32 devices in a mesh: doc: 8 (over z, x), tensor: 4 (over y, core).
Axes of the slice: x: 2, y: 2, z: 4, core: 2. Of those that a mesh axis runs over, the one named last changes fastest.
Arguments:
- hidden: bfloat16 [2048, 14336], P('doc', 'tensor'), may hold values from -33 to 33
- grads: bfloat16 [2048, 4096], P('doc'), may hold values from -61 to 61
- lengths: int32 [16], P('doc'), may hold values from 64 to 128, as said below
Outputs:
- grad_weight: float32 [4096, 14336], P('doc', 'tensor')
- norm_ratio: float32 [16], P('doc')
The draws below stay inside these ranges and needn't reach their ends.
Inputs may be any that keep to these rules, and one draw needn't show every extreme that they name: `lengths`: the valid tokens of a document are the first ones of its slot; some document fills its slot.
All inputs are finite; a program needn't handle non-finite values.
Results may differ from the reference program's by a relative error of at most 0.0003.
Values may be sent and summed in bfloat16 or wider, within the bound.
A program may use at most 128 MiB of HBM per device.

```python
import math
import jax
import jax.numpy as jnp
from jax import lax

D = 4096
FF = 14336
SLOT = 128
DOC_DEV = 2
DOCS = 16


def draw_hidden(key, part):
    subkeys = jax.random.split(key, 3)
    col_pos = jnp.arange(FF, dtype=jnp.float32) / FF
    col_scale = (0.6 + 1.2 * col_pos) * jnp.exp(jax.random.uniform(subkeys[0], (FF,), jnp.float32, math.log(0.5), math.log(2.0)))
    row_scale = jnp.exp(jax.random.uniform(subkeys[1], (DOCS * SLOT, 1), jnp.float32, math.log(0.5), math.log(2.0)))
    entries = jax.random.normal(subkeys[2], (DOCS * SLOT, FF), jnp.float32)
    entries = jnp.clip(entries, -4.5, 4.5)
    return (entries * row_scale * col_scale[None, :]).astype(jnp.bfloat16)


def draw_grads(key, part):
    subkeys = jax.random.split(key, 4)
    col_scale = jnp.exp(jax.random.uniform(subkeys[0], (D,), jnp.float32, math.log(0.5), math.log(2.0)))
    row_scale = jnp.exp(jax.random.uniform(subkeys[1], (DOCS, SLOT, 1), jnp.float32, math.log(0.5), math.log(2.0)))
    doc_scale = jnp.exp(jax.random.uniform(subkeys[2], (DOCS, 1, 1), jnp.float32, 0.0, math.log(10.0)))
    entries = jax.random.normal(subkeys[3], (DOCS, SLOT, D), jnp.float32)
    entries = jnp.clip(entries, -4.5, 4.5)
    scaled = entries * row_scale * doc_scale * col_scale[None, None, :] / 3.0
    return scaled.reshape(DOCS * SLOT, D).astype(jnp.bfloat16)


def draw_lengths(key, part):
    subkeys = jax.random.split(jax.random.fold_in(key, 17), 2)
    drawn = jax.random.randint(subkeys[0], (DOCS,), SLOT // 2, SLOT + 1, jnp.int32)
    chosen = jax.random.randint(subkeys[1], (), 0, DOCS, jnp.int32)
    return jnp.where(jnp.arange(DOCS, dtype=jnp.int32) == chosen, jnp.int32(SLOT), drawn)


def setup_inputs(seed: int = 0) -> dict:
    seeds = jax.random.split(jax.random.key(seed), 4)
    hidden = draw_hidden(jax.random.fold_in(seeds[3], 71), 0)
    grads = draw_grads(jax.random.fold_in(seeds[3], 71), 0)
    lengths = draw_lengths(jax.random.fold_in(seeds[3], 71), 0)
    return {"hidden": hidden, "grads": grads, "lengths": lengths}


clip_ratio = 2.0
epsilon = 1e-06

def weighted_sum(grad_blocks, hidden_blocks, weights):

    def step_fn(running, inputs):
        grad_one, hidden_one, weight_one = inputs
        product = lax.dot_general(grad_one, hidden_one, (((0,), (0,)), ((), ())), preferred_element_type=jnp.float32)
        return (running + weight_one * product, None)
    start_value = jnp.zeros((grad_blocks.shape[2], hidden_blocks.shape[2]), jnp.float32)
    running, unused = lax.scan(step_fn, start_value, (grad_blocks, hidden_blocks, weights))
    return running

def reference(hidden, grads, lengths):
    doc_count = lengths.shape[0]
    hidden_docs = hidden.reshape(doc_count, SLOT, FF)
    positions = jnp.arange(SLOT, dtype=jnp.int32)
    in_length = positions[None, :] < lengths[:, None]
    grad_docs = jnp.where(in_length[:, :, None], grads.reshape(doc_count, SLOT, D), jnp.zeros((), grads.dtype))

    def doc_square(pair):
        hidden_one, grad_one = pair
        hidden_gram = jnp.dot(hidden_one, hidden_one.T, preferred_element_type=jnp.float32)
        grad_gram = jnp.dot(grad_one, grad_one.T, preferred_element_type=jnp.float32)
        return jnp.sum(hidden_gram * grad_gram)
    squares = lax.map(doc_square, (hidden_docs, grad_docs))
    clip_norm = clip_ratio * math.sqrt(SLOT * FF * D)
    norm_ratio = jnp.sqrt(squares + epsilon) / clip_norm
    weights = jnp.minimum(1.0, 1.0 / norm_ratio) / (clip_ratio * math.sqrt(SLOT * doc_count))
    groups = doc_count // DOC_DEV

    def group_step(running, inputs):
        grad_group, hidden_group, weight_group = inputs
        part_sum = weighted_sum(grad_group, hidden_group, weight_group)
        return (running + part_sum, None)
    start_value = jnp.zeros((D, FF), jnp.float32)
    grad_weight, unused = lax.scan(group_step, start_value, (grad_docs.reshape(groups, DOC_DEV, SLOT, D), hidden_docs.reshape(groups, DOC_DEV, SLOT, FF), weights.reshape(groups, DOC_DEV)))
    return (grad_weight, norm_ratio)
```

```python
import functools
import math

import jax
import jax.numpy as jnp
from jax import lax
from jax.experimental import pallas as pl
from jax.experimental.pallas import tpu as pltpu
from jax.sharding import PartitionSpec as P

D = 4096
FF = 14336
SLOT = 128

clip_ratio = 2.0
epsilon = 1e-06
MESH = pl.DeviceIdType.MESH


def kernel(cfg, len_ref, hid, grads, out, nr_ref, G, gv, mrx, mT, acc, sq, wts,
           lsem, gsem, osem, ssem, rsem, ms_s, ms_r, m2_s, m2_r, sq_s, sq_r, w_s, w_r):
    nz, nx, T, C, docs, n_docs = cfg
    n = nz * nx
    me = lax.axis_index("doc")
    t = lax.axis_index("tensor")
    z, x = me // nx, lax.rem(me, nx)
    W = G.shape[3]
    R = G.shape[2]
    Dl = acc.shape[1]
    q = R // T
    trow = pl.ds(pl.multiple_of(t * q, q), q)

    for c in range(C):
        pltpu.make_async_copy(hid.at[:, pl.ds(c * W, W)], G.at[c, me], lsem.at[c]).start()
    pltpu.make_async_copy(grads, gv, gsem).start()

    bar = pltpu.get_barrier_semaphore()
    for k in range(1, n):
        pl.semaphore_signal(bar, inc=1, device_id={"doc": lax.rem(me + k, n), "tensor": t},
                            device_id_type=MESH)
    for k in range(1, T):
        pl.semaphore_signal(bar, inc=1, device_id={"doc": me, "tensor": lax.rem(t + k, T)},
                            device_id_type=MESH)
    pl.semaphore_wait(bar, n - 1 + T - 1)

    def block(s, c, k, to):
        return pltpu.make_async_remote_copy(
            src_ref=G.at[c, s], dst_ref=G.at[c, s], send_sem=ssem.at[s, c, k],
            recv_sem=rsem.at[s, c], device_id={"doc": to, "tensor": t}, device_id_type=MESH)

    up = jnp.minimum(me + nx, n - nx + x)
    down = jnp.maximum(me - nx, x)

    def send_up(s, c):
        @pl.when(z < nz - 1)
        def _():
            block(s, c, 0, up).start()

    def send_down(s, c):
        @pl.when(z > 0)
        def _():
            block(s, c, 1, down).start()

    def send_x(s, c):
        for k in range(1, nx):
            block(s, c, 1 + k, z * nx + lax.rem(x + k, nx)).start()

    def arrive(s, c):
        block(s, c, 0, up).wait_recv()

    for c in range(C):
        pltpu.make_async_copy(hid.at[:, pl.ds(c * W, W)], G.at[c, me], lsem.at[c]).wait()
        send_x(me, c)
        send_up(me, c)
        send_down(me, c)

    pltpu.make_async_copy(grads, gv, gsem).wait()
    for d in range(docs):
        keep = lax.broadcasted_iota(jnp.int32, (SLOT, 512), 0) < len_ref[d]

        @pl.loop(0, gv.shape[1] // 512)
        def _(i):
            cols = pl.ds(pl.multiple_of(i * 512, 512), 512)
            v = gv[d * SLOT:(d + 1) * SLOT, cols]
            gv[d * SLOT:(d + 1) * SLOT, cols] = jnp.where(
                keep, v.astype(jnp.float32), 0.0).astype(v.dtype)

    def share(j, s):
        return pltpu.make_async_remote_copy(
            src_ref=gv.at[trow, pl.ds(pl.multiple_of(j * Dl, Dl), Dl)],
            dst_ref=mrx.at[s, trow, :], send_sem=ms_s.at[j], recv_sem=ms_r.at[s],
            device_id={"doc": j, "tensor": t}, device_id_type=MESH)

    for k in range(1, n):
        share(lax.rem(me + k, n), me).start()

    def nt(a, b):
        return lax.dot_general(a, b, (((1,), (1,)), ((), ())),
                               preferred_element_type=jnp.float32)

    row = lax.broadcasted_iota(jnp.int32, (8, 128), 0)
    part = jnp.zeros((8, 128), jnp.float32)
    zero = jnp.zeros((SLOT, SLOT), jnp.float32)
    for d in range(docs):
        rows = slice(d * SLOT, (d + 1) * SLOT)

        def hid_step(c, run):
            h = G[c, me, rows, :]
            return run + nt(h, h)

        def grad_step(i, run):
            m = gv[rows, pl.ds(pl.multiple_of(i * 512, 512), 512)]
            return run + nt(m, m)

        hg = lax.fori_loop(0, C, hid_step, zero)
        gg = lax.fori_loop(0, gv.shape[1] // 512, grad_step, zero)
        one = jnp.sum(jnp.sum(hg * gg, axis=1, keepdims=True), axis=0, keepdims=True)
        part = jnp.where(row == d, one, part)
    sq[t] = part

    def sq_copy(tt, src):
        return pltpu.make_async_remote_copy(
            src_ref=sq.at[src], dst_ref=sq.at[src], send_sem=sq_s.at[tt],
            recv_sem=sq_r.at[src], device_id={"doc": me, "tensor": tt}, device_id_type=MESH)

    for k in range(1, T):
        sq_copy(lax.rem(t + k, T), t).start()
    mT[me] = gv[:, pl.ds(pl.multiple_of(me * Dl, Dl), Dl)].T
    for k in range(1, T):
        o = lax.rem(t + k, T)
        sq_copy(o, o).wait_recv()
    total = sq[0]
    for k in range(1, T):
        total = total + sq[k]
    clip_norm = clip_ratio * math.sqrt(SLOT * FF * D)
    ratio = jnp.sqrt(total + epsilon) / clip_norm
    nr_ref[...] = ratio
    wts[me] = jnp.minimum(1.0, 1.0 / ratio) / (clip_ratio * math.sqrt(SLOT * n_docs))

    def w_copy(j, s):
        return pltpu.make_async_remote_copy(
            src_ref=wts.at[s], dst_ref=wts.at[s], send_sem=w_s.at[j], recv_sem=w_r.at[s],
            device_id={"doc": j, "tensor": t}, device_id_type=MESH)

    for k in range(1, n):
        w_copy(lax.rem(me + k, n), me).start()

    def spread(s, tt, o):
        rr = pl.ds(pl.multiple_of(o * q, q), q)
        return pltpu.make_async_remote_copy(
            src_ref=mrx.at[s, rr, :], dst_ref=mrx.at[s, rr, :], send_sem=m2_s.at[s, tt],
            recv_sem=m2_r.at[s, o], device_id={"doc": me, "tensor": tt}, device_id_type=MESH)

    @pl.loop(1, n)
    def _(k):
        s = lax.rem(me + k, n)
        share(s, s).wait_recv()
        for kk in range(1, T):
            spread(s, lax.rem(t + kk, T), t).start()

    def product(s, c, first):
        tile = min(256, Dl)
        for r in range(Dl // tile):
            rr = slice(r * tile, (r + 1) * tile)
            tot = None
            for d in range(docs):
                p = jnp.dot(mT[s, rr, d * SLOT:(d + 1) * SLOT],
                            G[c, s, d * SLOT:(d + 1) * SLOT, :],
                            preferred_element_type=jnp.float32)
                p = p * wts[s, d:d + 1, 0:1]
                tot = p if tot is None else tot + p
            acc[c, rr, :] = tot if first else acc[c, rr, :] + tot

    @pl.loop(0, C)
    def _(c):
        product(me, c, True)

    for k in range(1, nx):
        s = z * nx + lax.rem(x + k, nx)
        arrive(s, 0)
        send_up(s, 0)
        send_down(s, 0)

    @pl.loop(1, n)
    def _(k):
        s = lax.rem(me + k, n)
        for kk in range(1, T):
            o = lax.rem(t + kk, T)
            spread(s, o, o).wait_recv()
        w_copy(s, s).wait_recv()
        mT[s] = mrx[s].T

    def out_copy(c):
        return pltpu.make_async_copy(acc.at[c], out.at[:, pl.ds(pl.multiple_of(c * W, W), W)],
                                     osem.at[c])

    for dist in range(1, nz + 1):
        def step(c, dist=dist):
            if dist < nz:
                for sign, send in ((-1, send_up), (1, send_down)):
                    sz = z + sign * dist

                    @pl.when((sz >= 0) & (sz < nz))
                    def _():
                        s = sz * nx + x
                        arrive(s, c)
                        send(s, c)

                        @pl.when(c > 0)
                        def _():
                            send_x(s, c)

                        @pl.when(c == 0)
                        def _():
                            for k in range(1, nx):
                                s2 = sz * nx + lax.rem(x + k, nx)
                                arrive(s2, 0)
                                send(s2, 0)
                                product(s2, 0, False)

                        product(s, c, False)
            for sign in ((-1, 1) if dist > 1 else (1,)):
                sz = z + sign * (dist - 1)

                @pl.when((sz >= 0) & (sz < nz))
                def _():
                    for k in range(1, nx):
                        s = sz * nx + lax.rem(x + k, nx)
                        if dist == 1:
                            @pl.when(c > 0)
                            def _():
                                arrive(s, c)
                            product(s, c, False)
                        else:
                            @pl.when(c > 0)
                            def _():
                                arrive(s, c)
                                product(s, c, False)
            if dist == nz:
                out_copy(c).start()

        pl.loop(0, C)(step)

    for k in range(1, T):
        sq_copy(lax.rem(t + k, T), t).wait_send()

    @pl.loop(1, n)
    def _(k):
        j = lax.rem(me + k, n)
        share(j, me).wait_send()
        w_copy(j, me).wait_send()
        for kk in range(1, T):
            spread(j, lax.rem(t + kk, T), t).wait_send()

    @pl.loop(0, n)
    def _(s):
        sz, sx = s // nx, lax.rem(s, nx)

        @pl.loop(0, C)
        def _(c):
            along = (sx == x) | (c == 0)

            @pl.when(along & (z < nz - 1) & (sz <= z))
            def _():
                block(s, c, 0, up).wait_send()

            @pl.when(along & (z > 0) & (sz >= z))
            def _():
                block(s, c, 1, down).wait_send()

            @pl.when((sx == x) & ((c > 0) | (sz == z)))
            def _():
                for k in range(1, nx):
                    block(s, c, 1 + k, z * nx + lax.rem(x + k, nx)).wait_send()

    @pl.loop(0, C)
    def _(c):
        out_copy(c).wait()


def per_device(hidden, grads, lengths, *, n, T):
    docs = lengths.shape[0]
    R, ffl = hidden.shape
    dm = grads.shape[1]
    Dl = dm // n
    nx = max(k for k in range(1, n + 1) if n % k == 0 and k * k <= n)
    nz = n // nx
    C = next(k for k in (7, 8, 4, 2, 1) if ffl % (128 * k) == 0)
    W = ffl // C
    dma = pltpu.SemaphoreType.DMA
    f32, bf16 = jnp.float32, hidden.dtype
    gw, nr = pl.pallas_call(
        functools.partial(kernel, (nz, nx, T, C, docs, docs * n)),
        out_shape=(jax.ShapeDtypeStruct((Dl, ffl), f32), jax.ShapeDtypeStruct((8, 128), f32)),
        in_specs=[pl.BlockSpec(memory_space=pltpu.SMEM), pl.BlockSpec(memory_space=pl.ANY),
                  pl.BlockSpec(memory_space=pl.ANY)],
        out_specs=(pl.BlockSpec(memory_space=pl.ANY), pl.BlockSpec(memory_space=pltpu.VMEM)),
        scratch_shapes=[
            pltpu.VMEM((C, n, R, W), bf16),
            pltpu.VMEM((R, dm), bf16),
            pltpu.VMEM((n, R, Dl), bf16),
            pltpu.VMEM((n, Dl, R), bf16),
            pltpu.VMEM((C, Dl, W), f32),
            pltpu.VMEM((T, 8, 128), f32),
            pltpu.VMEM((n, 8, 128), f32),
            dma((C,)), dma, dma((C,)),
            dma((n, C, 1 + nx)), dma((n, C)),
            dma((n,)), dma((n,)), dma((n, T)), dma((n, T)),
            dma((T,)), dma((T,)), dma((n,)), dma((n,)),
        ],
        compiler_params=pltpu.CompilerParams(
            collective_id=0, has_side_effects=True, vmem_limit_bytes=56 * 2**20),
        cost_estimate=pl.CostEstimate(flops=2 * R * n * Dl * ffl, transcendentals=0,
                                      bytes_accessed=4 * Dl * ffl + 2 * R * (ffl + dm)),
    )(lengths, hidden, grads)
    return gw, nr[:docs, 0]


def solution(mesh):
    in_specs = (P("doc", "tensor"), P("doc", None), P("doc"))
    out_specs = (P("doc", "tensor"), P("doc"))
    body = functools.partial(per_device, n=mesh.shape["doc"], T=mesh.shape["tensor"])
    return jax.shard_map(
        body, mesh=mesh, in_specs=in_specs, out_specs=out_specs, check_vma=False
    )
```

```python
import functools
import math

import jax
import jax.numpy as jnp
from jax import lax
from jax.experimental import pallas as pl
from jax.experimental.pallas import tpu as pltpu
from jax.sharding import PartitionSpec as P

D = 4096
FF = 14336
SLOT = 128

clip_ratio = 2.0
epsilon = 1e-06
MESH = pl.DeviceIdType.MESH


def kernel(cfg, len_ref, hid, grads, out, nr_ref, G, gv, mrx, mT, acc, sq, wts,
           lsem, gsem, osem, ssem, rsem, ms_s, ms_r, m2_s, m2_r, sq_s, sq_r, w_s, w_r):
    nz, nx, T, C, dup, docs, n_docs = cfg
    n = nz * nx
    me = lax.axis_index("doc")
    t = lax.axis_index("tensor")
    z, x = me // nx, lax.rem(me, nx)
    W = G.shape[3]
    R = G.shape[2]
    Dl = acc.shape[1]
    q = R // T
    early = min(3, C)
    trow = pl.ds(pl.multiple_of(t * q, q), q)

    for c in range(C):
        pltpu.make_async_copy(hid.at[:, pl.ds(c * W, W)], G.at[c, me], lsem.at[c]).start()
    pltpu.make_async_copy(grads, gv, gsem).start()

    bar = pltpu.get_barrier_semaphore()
    for k in range(1, n):
        pl.semaphore_signal(bar, inc=1, device_id={"doc": lax.rem(me + k, n), "tensor": t},
                            device_id_type=MESH)
    for k in range(1, T):
        pl.semaphore_signal(bar, inc=1, device_id={"doc": me, "tensor": lax.rem(t + k, T)},
                            device_id_type=MESH)
    pl.semaphore_wait(bar, n - 1 + T - 1)

    def block(s, c, k, to):
        return pltpu.make_async_remote_copy(
            src_ref=G.at[c, s], dst_ref=G.at[c, s], send_sem=ssem.at[s, c, k],
            recv_sem=rsem.at[s, c], device_id={"doc": to, "tensor": t}, device_id_type=MESH)

    up = jnp.minimum(me + nx, n - nx + x)
    down = jnp.maximum(me - nx, x)

    def send_up(s, c):
        @pl.when(z < nz - 1)
        def _():
            block(s, c, 0, up).start()

    def send_down(s, c):
        @pl.when(z > 0)
        def _():
            block(s, c, 1, down).start()

    def send_x(s, c):
        for k in range(1, nx):
            block(s, c, 1 + k, z * nx + lax.rem(x + k, nx)).start()

    def arrive(s, c):
        block(s, c, 0, up).wait_recv()

    def land(c):
        pltpu.make_async_copy(hid.at[:, pl.ds(c * W, W)], G.at[c, me], lsem.at[c]).wait()

    def send_own(c):
        send_x(me, c)
        send_up(me, c)
        send_down(me, c)

    for c in range(early):
        land(c)
        send_own(c)

    pltpu.make_async_copy(grads, gv, gsem).wait()
    for d in range(docs):
        keep = lax.broadcasted_iota(jnp.int32, (SLOT, 512), 0) < len_ref[d]

        @pl.loop(0, gv.shape[1] // 512)
        def _(i):
            cols = pl.ds(pl.multiple_of(i * 512, 512), 512)
            v = gv[d * SLOT:(d + 1) * SLOT, cols]
            gv[d * SLOT:(d + 1) * SLOT, cols] = jnp.where(
                keep, v.astype(jnp.float32), 0.0).astype(v.dtype)

    def share(j, s):
        return pltpu.make_async_remote_copy(
            src_ref=gv.at[trow, pl.ds(pl.multiple_of(j * Dl, Dl), Dl)],
            dst_ref=mrx.at[s, trow, :], send_sem=ms_s.at[j], recv_sem=ms_r.at[s],
            device_id={"doc": j, "tensor": t}, device_id_type=MESH)

    for k in range(1, n):
        share(lax.rem(me + k, n), me).start()

    def nt(a, b):
        return lax.dot_general(a, b, (((1,), (1,)), ((), ())),
                               preferred_element_type=jnp.float32)

    for c in range(early, C):
        land(c)
    row = lax.broadcasted_iota(jnp.int32, (8, 128), 0)
    part = jnp.zeros((8, 128), jnp.float32)
    zero = jnp.zeros((SLOT, SLOT), jnp.float32)
    for d in range(docs):
        rows = slice(d * SLOT, (d + 1) * SLOT)

        def hid_step(c, run):
            h = G[c, me, rows, :]
            return run + nt(h, h)

        def grad_step(i, run):
            m = gv[rows, pl.ds(pl.multiple_of(i * 512, 512), 512)]
            return run + nt(m, m)

        hg = lax.fori_loop(0, C, hid_step, zero)
        gg = lax.fori_loop(0, gv.shape[1] // 512, grad_step, zero)
        one = jnp.sum(jnp.sum(hg * gg, axis=1, keepdims=True), axis=0, keepdims=True)
        part = jnp.where(row == d, one, part)
    sq[t] = part

    def sq_copy(tt, src):
        return pltpu.make_async_remote_copy(
            src_ref=sq.at[src], dst_ref=sq.at[src], send_sem=sq_s.at[tt],
            recv_sem=sq_r.at[src], device_id={"doc": me, "tensor": tt}, device_id_type=MESH)

    for k in range(1, T):
        sq_copy(lax.rem(t + k, T), t).start()
    mT[me] = gv[:, pl.ds(pl.multiple_of(me * Dl, Dl), Dl)].T
    for k in range(1, T):
        o = lax.rem(t + k, T)
        sq_copy(o, o).wait_recv()
    total = sq[0]
    for k in range(1, T):
        total = total + sq[k]
    clip_norm = clip_ratio * math.sqrt(SLOT * FF * D)
    ratio = jnp.sqrt(total + epsilon) / clip_norm
    nr_ref[...] = ratio
    wts[me] = jnp.minimum(1.0, 1.0 / ratio) / (clip_ratio * math.sqrt(SLOT * n_docs))

    def w_copy(j, s):
        return pltpu.make_async_remote_copy(
            src_ref=wts.at[s], dst_ref=wts.at[s], send_sem=w_s.at[j], recv_sem=w_r.at[s],
            device_id={"doc": j, "tensor": t}, device_id_type=MESH)

    for k in range(1, n):
        w_copy(lax.rem(me + k, n), me).start()
    for c in range(early, C):
        send_own(c)

    def spread(s, tt, o):
        rr = pl.ds(pl.multiple_of(o * q, q), q)
        return pltpu.make_async_remote_copy(
            src_ref=mrx.at[s, rr, :], dst_ref=mrx.at[s, rr, :], send_sem=m2_s.at[s, tt],
            recv_sem=m2_r.at[s, o], device_id={"doc": me, "tensor": tt}, device_id_type=MESH)

    def product(s, c, first):
        tile = min(256, Dl)
        for r in range(Dl // tile):
            rr = slice(r * tile, (r + 1) * tile)
            tot = None
            for d in range(docs):
                p = jnp.dot(mT[s, rr, d * SLOT:(d + 1) * SLOT],
                            G[c, s, d * SLOT:(d + 1) * SLOT, :],
                            preferred_element_type=jnp.float32)
                p = p * wts[s, d:d + 1, 0:1]
                tot = p if tot is None else tot + p
            acc[c, rr, :] = tot if first else acc[c, rr, :] + tot

    for k in range(1, nx):
        s = z * nx + lax.rem(x + k, nx)
        for c in range(dup):
            arrive(s, c)
            send_up(s, c)
            send_down(s, c)

    def out_copy(c):
        return pltpu.make_async_copy(acc.at[c], out.at[:, pl.ds(pl.multiple_of(c * W, W), W)],
                                     osem.at[c])

    def each_side(dist, fn):
        for sign, send in ((-1, send_up), (1, send_down)):
            sz = z + sign * dist

            @pl.when((sz >= 0) & (sz < nz))
            def _():
                fn(sz, send)

    def forward(dist, c):
        def one(sz, send):
            s = sz * nx + x
            arrive(s, c)
            send(s, c)

            @pl.when(c >= dup)
            def _():
                send_x(s, c)

            @pl.when(c < dup)
            def _():
                for k in range(1, nx):
                    s2 = sz * nx + lax.rem(x + k, nx)
                    arrive(s2, c)
                    send(s2, c)

        each_side(dist, one)

    def multiply(dist, c):
        def one(sz, send):
            product(sz * nx + x, c, False)
            for k in range(1, nx):
                s = sz * nx + lax.rem(x + k, nx)

                @pl.when(c >= dup)
                def _():
                    arrive(s, c)

                product(s, c, False)

        if dist:
            each_side(dist, one)
        else:
            product(me, c, True)
            for k in range(1, nx):
                s = z * nx + lax.rem(x + k, nx)

                @pl.when(c >= dup)
                def _():
                    arrive(s, c)

                product(s, c, False)

    @pl.loop(0, C)
    def _(c):
        forward(1, c)

    @pl.loop(1, n)
    def _(k):
        s = lax.rem(me + k, n)
        share(s, s).wait_recv()
        for kk in range(1, T):
            spread(s, lax.rem(t + kk, T), t).start()

    @pl.loop(1, n)
    def _(k):
        s = lax.rem(me + k, n)
        for kk in range(1, T):
            o = lax.rem(t + kk, T)
            spread(s, o, o).wait_recv()
        w_copy(s, s).wait_recv()
        mT[s] = mrx[s].T

    for dist in range(2, nz + 1):
        def step(c, dist=dist):
            if dist < nz:
                forward(dist, c)
            if dist == 2:
                multiply(0, c)
            multiply(dist - 1, c)
            if dist == nz:
                out_copy(c).start()

        pl.loop(0, C)(step)

    for k in range(1, T):
        sq_copy(lax.rem(t + k, T), t).wait_send()

    @pl.loop(1, n)
    def _(k):
        j = lax.rem(me + k, n)
        share(j, me).wait_send()
        w_copy(j, me).wait_send()
        for kk in range(1, T):
            spread(j, lax.rem(t + kk, T), t).wait_send()

    @pl.loop(0, n)
    def _(s):
        sz, sx = s // nx, lax.rem(s, nx)

        @pl.loop(0, C)
        def _(c):
            along = (sx == x) | (c < dup)

            @pl.when(along & (z < nz - 1) & (sz <= z))
            def _():
                block(s, c, 0, up).wait_send()

            @pl.when(along & (z > 0) & (sz >= z))
            def _():
                block(s, c, 1, down).wait_send()

            @pl.when((sx == x) & ((c >= dup) | (sz == z)))
            def _():
                for k in range(1, nx):
                    block(s, c, 1 + k, z * nx + lax.rem(x + k, nx)).wait_send()

    @pl.loop(0, C)
    def _(c):
        out_copy(c).wait()


def per_device(hidden, grads, lengths, *, n, T):
    docs = lengths.shape[0]
    R, ffl = hidden.shape
    dm = grads.shape[1]
    Dl = dm // n
    nx = max(k for k in range(1, n + 1) if n % k == 0 and k * k <= n)
    nz = n // nx
    C = next(k for k in (7, 8, 4, 2, 1) if ffl % (128 * k) == 0)
    dup = C // 7
    W = ffl // C
    dma = pltpu.SemaphoreType.DMA
    f32, bf16 = jnp.float32, hidden.dtype
    gw, nr = pl.pallas_call(
        functools.partial(kernel, (nz, nx, T, C, dup, docs, docs * n)),
        out_shape=(jax.ShapeDtypeStruct((Dl, ffl), f32), jax.ShapeDtypeStruct((8, 128), f32)),
        in_specs=[pl.BlockSpec(memory_space=pltpu.SMEM), pl.BlockSpec(memory_space=pl.ANY),
                  pl.BlockSpec(memory_space=pl.ANY)],
        out_specs=(pl.BlockSpec(memory_space=pl.ANY), pl.BlockSpec(memory_space=pltpu.VMEM)),
        scratch_shapes=[
            pltpu.VMEM((C, n, R, W), bf16),
            pltpu.VMEM((R, dm), bf16),
            pltpu.VMEM((n, R, Dl), bf16),
            pltpu.VMEM((n, Dl, R), bf16),
            pltpu.VMEM((C, Dl, W), f32),
            pltpu.VMEM((T, 8, 128), f32),
            pltpu.VMEM((n, 8, 128), f32),
            dma((C,)), dma, dma((C,)),
            dma((n, C, 1 + nx)), dma((n, C)),
            dma((n,)), dma((n,)), dma((n, T)), dma((n, T)),
            dma((T,)), dma((T,)), dma((n,)), dma((n,)),
        ],
        compiler_params=pltpu.CompilerParams(
            collective_id=0, has_side_effects=True, vmem_limit_bytes=40 * 2**20),
        cost_estimate=pl.CostEstimate(flops=2 * R * n * Dl * ffl, transcendentals=0,
                                      bytes_accessed=4 * Dl * ffl + 2 * R * (ffl + dm)),
    )(lengths, hidden, grads)
    return gw, nr[:docs, 0]


def solution(mesh):
    in_specs = (P("doc", "tensor"), P("doc", None), P("doc"))
    out_specs = (P("doc", "tensor"), P("doc"))
    body = functools.partial(per_device, n=mesh.shape["doc"], T=mesh.shape["tensor"])
    return jax.shard_map(
        body, mesh=mesh, in_specs=in_specs, out_specs=out_specs, check_vma=False
    )
```

```python
import functools
import math

import jax
import jax.numpy as jnp
from jax import lax
from jax.experimental import pallas as pl
from jax.experimental.pallas import tpu as pltpu
from jax.sharding import PartitionSpec as P

D = 4096
FF = 14336
SLOT = 128

clip_ratio = 2.0
epsilon = 1e-06
MESH = pl.DeviceIdType.MESH


def kernel(cfg, len_ref, hid, grads, out, nr_ref, G, gv, mrx, mT, acc, sq, wts,
           lsem, gsem, osem, ssem, rsem, ms_s, ms_r, m2_s, m2_r, sq_s, sq_r, w_s, w_r):
    nz, nx, T, C, dup, docs, n_docs = cfg
    n = nz * nx
    me = lax.axis_index("doc")
    t = lax.axis_index("tensor")
    z, x = me // nx, lax.rem(me, nx)
    W = G.shape[3]
    R = G.shape[2]
    Dl = acc.shape[1]
    q = R // T
    early = min(3, C)
    trow = pl.ds(pl.multiple_of(t * q, q), q)

    for c in range(C):
        pltpu.make_async_copy(hid.at[:, pl.ds(c * W, W)], G.at[c, me], lsem.at[c]).start()
    pltpu.make_async_copy(grads, gv, gsem).start()

    bar = pltpu.get_barrier_semaphore()
    for k in range(1, n):
        pl.semaphore_signal(bar, inc=1, device_id={"doc": lax.rem(me + k, n), "tensor": t},
                            device_id_type=MESH)
    for k in range(1, T):
        pl.semaphore_signal(bar, inc=1, device_id={"doc": me, "tensor": lax.rem(t + k, T)},
                            device_id_type=MESH)
    pl.semaphore_wait(bar, n - 1 + T - 1)

    def block(s, c, k, to):
        return pltpu.make_async_remote_copy(
            src_ref=G.at[c, s], dst_ref=G.at[c, s], send_sem=ssem.at[s, c, k],
            recv_sem=rsem.at[s, c], device_id={"doc": to, "tensor": t}, device_id_type=MESH)

    up = jnp.minimum(me + nx, n - nx + x)
    down = jnp.maximum(me - nx, x)

    def send_up(s, c):
        @pl.when(z < nz - 1)
        def _():
            block(s, c, 0, up).start()

    def send_down(s, c):
        @pl.when(z > 0)
        def _():
            block(s, c, 1, down).start()

    def send_x(s, c):
        for k in range(1, nx):
            block(s, c, 1 + k, z * nx + lax.rem(x + k, nx)).start()

    def arrive(s, c):
        block(s, c, 0, up).wait_recv()

    def land(c):
        pltpu.make_async_copy(hid.at[:, pl.ds(c * W, W)], G.at[c, me], lsem.at[c]).wait()

    def send_own(c):
        send_x(me, c)
        send_up(me, c)
        send_down(me, c)

    for c in range(early):
        land(c)
        send_own(c)

    pltpu.make_async_copy(grads, gv, gsem).wait()
    for d in range(docs):
        keep = lax.broadcasted_iota(jnp.int32, (SLOT, 512), 0) < len_ref[d]

        @pl.loop(0, gv.shape[1] // 512)
        def _(i):
            cols = pl.ds(pl.multiple_of(i * 512, 512), 512)
            v = gv[d * SLOT:(d + 1) * SLOT, cols]
            gv[d * SLOT:(d + 1) * SLOT, cols] = jnp.where(
                keep, v.astype(jnp.float32), 0.0).astype(v.dtype)

    def share(j, s):
        return pltpu.make_async_remote_copy(
            src_ref=gv.at[trow, pl.ds(pl.multiple_of(j * Dl, Dl), Dl)],
            dst_ref=mrx.at[s, trow, :], send_sem=ms_s.at[j], recv_sem=ms_r.at[s],
            device_id={"doc": j, "tensor": t}, device_id_type=MESH)

    for k in range(1, n):
        share(lax.rem(me + k, n), me).start()

    def nt(a, b):
        return lax.dot_general(a, b, (((1,), (1,)), ((), ())),
                               preferred_element_type=jnp.float32)

    for c in range(early, C):
        land(c)
    row = lax.broadcasted_iota(jnp.int32, (8, 128), 0)
    part = jnp.zeros((8, 128), jnp.float32)
    zero = jnp.zeros((SLOT, SLOT), jnp.float32)
    for d in range(docs):
        rows = slice(d * SLOT, (d + 1) * SLOT)

        def hid_step(c, run):
            h = G[c, me, rows, :]
            return run + nt(h, h)

        def grad_step(i, run):
            m = gv[rows, pl.ds(pl.multiple_of(i * 512, 512), 512)]
            return run + nt(m, m)

        hg = lax.fori_loop(0, C, hid_step, zero)
        gg = lax.fori_loop(0, gv.shape[1] // 512, grad_step, zero)
        one = jnp.sum(jnp.sum(hg * gg, axis=1, keepdims=True), axis=0, keepdims=True)
        part = jnp.where(row == d, one, part)
    sq[t] = part

    def sq_copy(tt, src):
        return pltpu.make_async_remote_copy(
            src_ref=sq.at[src], dst_ref=sq.at[src], send_sem=sq_s.at[tt],
            recv_sem=sq_r.at[src], device_id={"doc": me, "tensor": tt}, device_id_type=MESH)

    for k in range(1, T):
        sq_copy(lax.rem(t + k, T), t).start()
    mT[me] = gv[:, pl.ds(pl.multiple_of(me * Dl, Dl), Dl)].T
    for k in range(1, T):
        o = lax.rem(t + k, T)
        sq_copy(o, o).wait_recv()
    total = sq[0]
    for k in range(1, T):
        total = total + sq[k]
    clip_norm = clip_ratio * math.sqrt(SLOT * FF * D)
    ratio = jnp.sqrt(total + epsilon) / clip_norm
    nr_ref[...] = ratio
    wts[me] = jnp.minimum(1.0, 1.0 / ratio) / (clip_ratio * math.sqrt(SLOT * n_docs))

    def w_copy(j, s):
        return pltpu.make_async_remote_copy(
            src_ref=wts.at[s], dst_ref=wts.at[s], send_sem=w_s.at[j], recv_sem=w_r.at[s],
            device_id={"doc": j, "tensor": t}, device_id_type=MESH)

    for k in range(1, n):
        w_copy(lax.rem(me + k, n), me).start()
    for c in range(early, C):
        send_own(c)

    def spread(s, tt, o):
        rr = pl.ds(pl.multiple_of(o * q, q), q)
        return pltpu.make_async_remote_copy(
            src_ref=mrx.at[s, rr, :], dst_ref=mrx.at[s, rr, :], send_sem=m2_s.at[s, tt],
            recv_sem=m2_r.at[s, o], device_id={"doc": me, "tensor": tt}, device_id_type=MESH)

    def product(s, c, first):
        tile = min(256, Dl)
        for r in range(Dl // tile):
            rr = slice(r * tile, (r + 1) * tile)
            tot = None
            for d in range(docs):
                p = jnp.dot(mT[s, rr, d * SLOT:(d + 1) * SLOT],
                            G[c, s, d * SLOT:(d + 1) * SLOT, :],
                            preferred_element_type=jnp.float32)
                p = p * wts[s, d:d + 1, 0:1]
                tot = p if tot is None else tot + p
            acc[c, rr, :] = tot if first else acc[c, rr, :] + tot

    for k in range(1, nx):
        s = z * nx + lax.rem(x + k, nx)
        for c in range(dup):
            arrive(s, c)
            send_up(s, c)
            send_down(s, c)

    def out_copy(c):
        return pltpu.make_async_copy(acc.at[c], out.at[:, pl.ds(pl.multiple_of(c * W, W), W)],
                                     osem.at[c])

    def each_side(dist, fn):
        for sign, send in ((-1, send_up), (1, send_down)):
            sz = z + sign * dist

            @pl.when((sz >= 0) & (sz < nz))
            def _():
                fn(sz, send)

    def forward(dist, c):
        def one(sz, send):
            s = sz * nx + x
            arrive(s, c)
            send(s, c)

            @pl.when(c >= dup)
            def _():
                send_x(s, c)

            @pl.when(c < dup)
            def _():
                for k in range(1, nx):
                    s2 = sz * nx + lax.rem(x + k, nx)
                    arrive(s2, c)
                    send(s2, c)

        each_side(dist, one)

    def multiply(dist, c):
        def one(sz, send):
            product(sz * nx + x, c, False)
            for k in range(1, nx):
                s = sz * nx + lax.rem(x + k, nx)

                @pl.when(c >= dup)
                def _():
                    arrive(s, c)

                product(s, c, False)

        if dist:
            each_side(dist, one)
        else:
            product(me, c, True)
            for k in range(1, nx):
                s = z * nx + lax.rem(x + k, nx)

                @pl.when(c >= dup)
                def _():
                    arrive(s, c)

                product(s, c, False)

    @pl.loop(0, C)
    def _(c):
        forward(1, c)

    @pl.loop(1, n)
    def _(k):
        s = lax.rem(me + k, n)
        share(s, s).wait_recv()
        for kk in range(1, T):
            spread(s, lax.rem(t + kk, T), t).start()

    @pl.loop(1, n)
    def _(k):
        s = lax.rem(me + k, n)
        for kk in range(1, T):
            o = lax.rem(t + kk, T)
            spread(s, o, o).wait_recv()
        w_copy(s, s).wait_recv()
        mT[s] = mrx[s].T

    for dist in range(2, nz + 1):
        def step(c, dist=dist):
            if dist < nz:
                forward(dist, c)
            if dist == 2:
                multiply(0, c)
            multiply(dist - 1, c)
            if dist == nz:
                out_copy(c).start()

        pl.loop(0, C)(step)

    for k in range(1, T):
        sq_copy(lax.rem(t + k, T), t).wait_send()

    @pl.loop(1, n)
    def _(k):
        j = lax.rem(me + k, n)
        share(j, me).wait_send()
        w_copy(j, me).wait_send()
        for kk in range(1, T):
            spread(j, lax.rem(t + kk, T), t).wait_send()

    @pl.loop(0, n)
    def _(s):
        sz, sx = s // nx, lax.rem(s, nx)

        @pl.loop(0, C)
        def _(c):
            along = (sx == x) | (c < dup)

            @pl.when(along & (z < nz - 1) & (sz <= z))
            def _():
                block(s, c, 0, up).wait_send()

            @pl.when(along & (z > 0) & (sz >= z))
            def _():
                block(s, c, 1, down).wait_send()

            @pl.when((sx == x) & ((c >= dup) | (sz == z)))
            def _():
                for k in range(1, nx):
                    block(s, c, 1 + k, z * nx + lax.rem(x + k, nx)).wait_send()

    @pl.loop(0, C)
    def _(c):
        out_copy(c).wait()


def per_device(hidden, grads, lengths, *, n, T):
    docs = lengths.shape[0]
    R, ffl = hidden.shape
    dm = grads.shape[1]
    Dl = dm // n
    nx = max(k for k in range(1, n + 1) if n % k == 0 and k * k <= n)
    nz = n // nx
    C = next(k for k in (7, 8, 4, 2, 1) if ffl % (128 * k) == 0)
    dup = C // 7
    W = ffl // C
    dma = pltpu.SemaphoreType.DMA
    f32, bf16 = jnp.float32, hidden.dtype
    gw, nr = pl.pallas_call(
        functools.partial(kernel, (nz, nx, T, C, dup, docs, docs * n)),
        out_shape=(jax.ShapeDtypeStruct((Dl, ffl), f32), jax.ShapeDtypeStruct((8, 128), f32)),
        in_specs=[pl.BlockSpec(memory_space=pltpu.SMEM), pl.BlockSpec(memory_space=pltpu.HBM),
                  pl.BlockSpec(memory_space=pltpu.HBM)],
        out_specs=(pl.BlockSpec(memory_space=pl.ANY), pl.BlockSpec(memory_space=pltpu.VMEM)),
        scratch_shapes=[
            pltpu.VMEM((C, n, R, W), bf16),
            pltpu.VMEM((R, dm), bf16),
            pltpu.VMEM((n, R, Dl), bf16),
            pltpu.VMEM((n, Dl, R), bf16),
            pltpu.VMEM((C, Dl, W), f32),
            pltpu.VMEM((T, 8, 128), f32),
            pltpu.VMEM((n, 8, 128), f32),
            dma((C,)), dma, dma((C,)),
            dma((n, C, 1 + nx)), dma((n, C)),
            dma((n,)), dma((n,)), dma((n, T)), dma((n, T)),
            dma((T,)), dma((T,)), dma((n,)), dma((n,)),
        ],
        compiler_params=pltpu.CompilerParams(
            collective_id=0, has_side_effects=True, vmem_limit_bytes=40 * 2**20),
        cost_estimate=pl.CostEstimate(flops=2 * R * n * Dl * ffl, transcendentals=0,
                                      bytes_accessed=4 * Dl * ffl + 2 * R * (ffl + dm)),
    )(lengths, pltpu.with_memory_space_constraint(hidden, pltpu.HBM), pltpu.with_memory_space_constraint(grads, pltpu.HBM))
    return gw, nr[:docs, 0]


def solution(mesh):
    in_specs = (P("doc", "tensor"), P("doc", None), P("doc"))
    out_specs = (P("doc", "tensor"), P("doc"))
    body = functools.partial(per_device, n=mesh.shape["doc"], T=mesh.shape["tensor"])
    return jax.shard_map(
        body, mesh=mesh, in_specs=in_specs, out_specs=out_specs, check_vma=False
    )
```
